32 devices in a mesh: grp: 2 (over y), ep: 16 (over z, x, core), sess: 1.
Axes of the slice: x: 2, y: 2, z: 4, core: 2. Of those that a mesh axis runs over, the one named last changes fastest.
Arguments:
- thinker_rows: bfloat16 [1024, 2048], P(('grp', 'ep', 'sess')), parts along dimension 0, may hold values from -6 to 6
- think_route: int32 [1024, 8], P(('grp', 'ep', 'sess')), parts along dimension 0, may hold values from 0 to 15, all different within a row; in each aligned block of 32 rows (0 to 31, 32 to 63, ...) at most 32 rows name the same one
- think_weight: float32 [1024, 8], P(('grp', 'ep', 'sess')), parts along dimension 0, may hold values from 0.1 to 1
- think_gate: bfloat16 [16, 2048, 768], P('ep', None, 'sess'), may hold values from -0.125 to 0.125
- think_up: bfloat16 [16, 2048, 768], P('ep', None, 'sess'), may hold values from -0.125 to 0.125
- think_down: bfloat16 [16, 768, 2048], P('ep', 'sess'), may hold values from -0.21875 to 0.21875
- proj_weight: bfloat16 [2048, 1024], P(None, 'sess'), may hold values from -0.125 to 0.125
- owner_map: int32 [1024], P(('grp', 'ep')), parts along dimension 0, may hold values from 0 to 31, as said below
- talk_gain: float32 [1024], replicated, may hold values from 0.5 to 1.5
- talk_route: int32 [1024, 6], P(('grp', 'ep', 'sess')), parts along dimension 0, may hold values from 0 to 15, all different within a row; in each aligned block of 32 rows (0 to 31, 32 to 63, ...) at most 24 rows name the same one
- talk_weight: float32 [1024, 6], P(('grp', 'ep', 'sess')), parts along dimension 0, may hold values from 0.1 to 1
- talk_gate: bfloat16 [16, 1024, 384], P(('ep', 'sess')), may hold values from -0.1875 to 0.1875
- talk_up: bfloat16 [16, 1024, 384], P(('ep', 'sess')), may hold values from -0.1875 to 0.1875
- talk_down: bfloat16 [16, 384, 1024], P(('ep', 'sess')), may hold values from -0.3125 to 0.3125
Outputs:
- thinker_branch: bfloat16 [1024, 2048], P(('grp', 'ep', 'sess')), parts along dimension 0
- talker_branch: bfloat16 [1024, 1024], P(('grp', 'ep', 'sess')), parts along dimension 0
The draws below stay inside these ranges and needn't reach their ends.
There are 2 independent parts, one for each index of `grp`. The reference program is written for one: setup_inputs(seed, part) draws one part's arguments, and reference() takes and returns one part's arrays. A program takes and returns all parts, laid end to end along the dimension named above; an argument that names none is the same for every part. Nothing has to cross between parts.
Inputs may be any that keep to these rules, and one draw needn't show every extreme that they name: `think_route`: within each aligned block of 32 rows (the rows of one device) no thinker expert is named by more than 32 rows, a bound that some block reaches. `talk_route`: within each aligned block of 32 rows (the rows of one device) no talker expert is named by more than 24 rows, a bound that some block reaches. `owner_map`: each aligned block of 32 entries holds every value of its range exactly once.
All inputs are finite; a program needn't handle non-finite values.
Results may differ from the reference program's by a relative error of at most 0.015.
Values may be sent and summed in bfloat16 or wider, within the bound.
A program may use at most 64 MiB of HBM per device.

```python
import math
import jax
import jax.numpy as jnp
import numpy as np
from jax import lax

D = 2048
FF_T = 768
TW = 1024
FF_K = 384
TOP_T = 8
TOP_K = 6
ROWS_DEV = 32
SESSIONS = 512
PAIR_ROWS = 32
EXPERTS_T = 16
EXPERTS_K = 16
CAP_T = 32
CAP_K = 24


def draw_owner_map(key, part):
    block_rows = PAIR_ROWS
    blocks = SESSIONS // block_rows
    keys = jax.random.split(jax.random.fold_in(key, 7), blocks)
    orders = jax.vmap(lambda single: jax.random.permutation(single, block_rows))(keys)
    return orders.reshape(SESSIONS).astype(jnp.int32)


def block_scale(key, shape, cuts, low, high):
    factor_of, own = 1.0, jax.random.fold_in(key, 6)
    for position, blocks in cuts:
        heights = jnp.exp(jax.random.uniform(jax.random.fold_in(own, position), (blocks,), jnp.float32, low / len(cuts), high / len(cuts)))
        factor_of = factor_of * jnp.repeat(heights, shape[position] // blocks).reshape([-1 if axis == position else 1 for axis in range(len(shape))])
    return factor_of


def assign_block(key, own, number, rows, number_of, top, bound, lean):
    sequence = jax.random.permutation(key, number_of)
    crowded, ordinary = shares(number_of, rows * top, bound, lean, True), shares(number_of, rows * top, bound, lean, False)
    places = jnp.arange(number_of)

    def named(lengths, turn):
        used = int((lengths > 0).sum())
        fixed = max(1, used // 4)
        moved = fixed + (places - fixed + turn * (used - fixed)) % max(1, number_of - fixed)
        return jnp.zeros((number_of,), jnp.int32).at[sequence[jnp.where(places < fixed, places, moved)]].set(jnp.asarray(lengths, jnp.int32))

    lengths = jnp.where(number % 4 == 0, named(crowded, number // 4), named(ordinary, number - number // 4 - 1))
    mixed = jax.random.permutation(jax.random.fold_in(own, 3), number_of)
    source_of, receiver = mixed[0:number_of // 2 * 2:2], mixed[1:number_of // 2 * 2:2]
    margin = jnp.minimum(lengths[source_of] - 1, bound - lengths[receiver]) // 2
    margin = jnp.where((source_of == sequence[0]) | (receiver == sequence[0]) | (lengths[receiver] == 0), 0, jnp.maximum(margin, 0))
    moved = jax.random.randint(jax.random.fold_in(own, 4), (number_of // 2,), 0, 1 << 20) % (margin + 1)
    lengths = lengths.at[source_of].add(-moved).at[receiver].add(moved)
    members = jnp.searchsorted(jnp.cumsum(lengths), jnp.arange(rows * top), side="right").astype(jnp.int32)
    grid = members.reshape(top, rows).T
    grid = grid[jax.random.permutation(jax.random.fold_in(own, 1), rows)]
    turn = jax.random.randint(jax.random.fold_in(own, 2), (rows, 1), 0, top)
    return jnp.take_along_axis(grid, (jnp.arange(top)[None, :] + turn) % top, axis=1)


def shares(number_of, total, reach, lean, full):
    loads = [(1 << 20) // math.isqrt(standing ** lean) + 1 for standing in range(1, number_of + 1)]
    largest = reach if full else min(reach, max(-(-total // number_of), total * loads[0] // sum(loads)))
    least = 1 if total - largest >= number_of - 1 else 0
    counts, spare = [largest] + [least] * (number_of - 1), total - largest - least * (number_of - 1)
    while spare > 0:
        candidates = [i for i in range(1, number_of) if counts[i] < largest] or [i for i in range(1, number_of) if counts[i] < reach]
        whole, left = sum([loads[i] for i in candidates]), spare
        for i in candidates:
            extra = min(reach - counts[i], max(1, left * loads[i] // whole), spare)
            counts[i] = counts[i] + extra
            spare = spare - extra
    return np.array(counts)


def centred(own_key, extent, width, bound, shards=(), held_as=jnp.bfloat16):
    level = block_scale(own_key, extent, shards, -0.22, 0.18) if shards else 1.0
    drawn = jax.random.normal(own_key, extent, jnp.float32) * width * level
    return jnp.minimum(jnp.maximum(drawn, -bound), bound).astype(held_as)


def setup_inputs(seed: int = 0, part: int = 0) -> dict:
    key_list = jax.random.split(jax.random.key(seed), 15)
    own_keys = jax.random.split(jax.random.fold_in(key_list[14], part), 15)
    thinker_rows = centred(own_keys[0], (SESSIONS, D), 1.0, 6.0, ((0, 16),))
    think_route_keys = jax.random.split(jax.random.fold_in(own_keys[1], 1), SESSIONS // ROWS_DEV)
    think_route_turns = jax.random.permutation(jax.random.fold_in(own_keys[1], 3), SESSIONS // ROWS_DEV)
    think_route = jax.vmap(lambda own, number: assign_block(jax.random.fold_in(own_keys[1], 2), own, number, ROWS_DEV, EXPERTS_T, TOP_T, CAP_T, 2))(think_route_keys, think_route_turns).reshape((SESSIONS, TOP_T))
    think_weight = jnp.clip(jnp.exp(math.log(1.0) - 2.3025851 * jax.random.uniform(own_keys[2], (SESSIONS, TOP_T), jnp.float32) ** block_scale(own_keys[2], (SESSIONS, TOP_T), ((0, 16),), -0.2, 0.2)), 0.1, 1.0)
    think_gate = centred(key_list[3], (EXPERTS_T, D, FF_T), D ** -0.5, 0.125, ((0, 16),))
    think_up = centred(key_list[4], (EXPERTS_T, D, FF_T), D ** -0.5, 0.125, ((0, 16),))
    think_down = centred(key_list[5], (EXPERTS_T, FF_T, D), FF_T ** -0.5, 0.21875, ((0, 16),))
    proj_weight = centred(key_list[6], (D, TW), D ** -0.5, 0.125)
    owner_map = draw_owner_map(jax.random.fold_in(jax.random.fold_in(key_list[14], part), 71), part)
    talk_gain = jnp.clip(1.0 + 0.1 * jax.random.normal(key_list[8], (TW,), jnp.float32), 0.5, 1.5)
    talk_route_keys = jax.random.split(jax.random.fold_in(own_keys[9], 1), SESSIONS // ROWS_DEV)
    talk_route_turns = jax.random.permutation(jax.random.fold_in(own_keys[9], 3), SESSIONS // ROWS_DEV)
    talk_route = jax.vmap(lambda own, number: assign_block(jax.random.fold_in(own_keys[9], 2), own, number, ROWS_DEV, EXPERTS_K, TOP_K, CAP_K, 2))(talk_route_keys, talk_route_turns).reshape((SESSIONS, TOP_K))
    talk_weight = jnp.clip(jnp.exp(math.log(1.0) - 2.3025851 * jax.random.uniform(own_keys[10], (SESSIONS, TOP_K), jnp.float32) ** block_scale(own_keys[10], (SESSIONS, TOP_K), ((0, 16),), -0.2, 0.2)), 0.1, 1.0)
    talk_gate = centred(key_list[11], (EXPERTS_K, TW, FF_K), TW ** -0.5, 0.1875, ((0, 16),))
    talk_up = centred(key_list[12], (EXPERTS_K, TW, FF_K), TW ** -0.5, 0.1875, ((0, 16),))
    talk_down = centred(key_list[13], (EXPERTS_K, FF_K, TW), FF_K ** -0.5, 0.3125, ((0, 16),))
    return {"thinker_rows": thinker_rows, "think_route": think_route, "think_weight": think_weight, "think_gate": think_gate, "think_up": think_up, "think_down": think_down, "proj_weight": proj_weight, "owner_map": owner_map, "talk_gain": talk_gain, "talk_route": talk_route, "talk_weight": talk_weight, "talk_gate": talk_gate, "talk_up": talk_up, "talk_down": talk_down}


def slot_places(route, rows_per, experts):
    sessions, picks = route.shape
    blocks = sessions // rows_per
    grouped = route.reshape(blocks, rows_per * picks)
    onehot = (grouped[:, :, None] == jnp.arange(experts, dtype=jnp.int32)[None, None, :]).astype(jnp.int32)
    before = jnp.cumsum(onehot, axis=1) - onehot
    return lax.optimization_barrier(jnp.sum(before * onehot, axis=2)).reshape(sessions * picks).astype(jnp.int32)

def mixture(row_block, route, weights, gate_w, up_w, down_w, rows_per, capacity):
    sessions, picks = route.shape
    experts = gate_w.shape[0]
    features = row_block.shape[1]
    blocks = sessions // rows_per
    places = slot_places(route, rows_per, experts)
    chosen = route.reshape(sessions * picks).astype(jnp.int32)
    owner_block = (jnp.arange(sessions * picks, dtype=jnp.int32) // (rows_per * picks)).astype(jnp.int32)
    target = chosen * (blocks * capacity) + owner_block * capacity + places
    copies = jnp.repeat(row_block, picks, axis=0)
    buffer = jnp.zeros((experts * blocks * capacity, features), row_block.dtype).at[target].set(copies)
    buffer = buffer.reshape(experts, blocks * capacity, features)

    def one_expert(operands):
        slab, gate_m, up_m, down_m = operands
        gate = jnp.dot(slab, gate_m, preferred_element_type=jnp.float32)
        upper = jnp.dot(slab, up_m, preferred_element_type=jnp.float32)
        hidden = (jax.nn.silu(gate) * upper).astype(jnp.bfloat16)
        return jnp.dot(hidden, down_m, preferred_element_type=jnp.float32).astype(jnp.bfloat16)
    outputs = lax.map(one_expert, (buffer, gate_w, up_w, down_w)).reshape(experts * blocks * capacity, features)
    gathered = outputs[target].astype(jnp.float32).reshape(sessions, picks, features)
    norm_weights = weights / lax.optimization_barrier(jnp.sum(weights, axis=1, keepdims=True))
    return lax.optimization_barrier(jnp.sum(gathered * norm_weights[:, :, None], axis=1)).astype(jnp.bfloat16)

def reference(thinker_rows, think_route, think_weight, think_gate, think_up, think_down, proj_weight, owner_map, talk_gain, talk_route, talk_weight, talk_gate, talk_up, talk_down):
    thinker_branch = mixture(thinker_rows, think_route, think_weight, think_gate, think_up, think_down, ROWS_DEV, CAP_T)
    projected = jnp.dot(thinker_branch, proj_weight, preferred_element_type=jnp.float32).astype(jnp.bfloat16)
    block_rows = PAIR_ROWS
    source = jnp.arange(SESSIONS, dtype=jnp.int32) // block_rows * block_rows + owner_map.astype(jnp.int32)
    relayed = projected[source].astype(jnp.float32)
    scale = lax.rsqrt(lax.optimization_barrier(jnp.mean(relayed * relayed, axis=1, keepdims=True)) + 1e-06)
    talk_rows = (relayed * scale * talk_gain[None, :]).astype(jnp.bfloat16)
    talker_branch = mixture(talk_rows, talk_route, talk_weight, talk_gate, talk_up, talk_down, ROWS_DEV, CAP_K)
    return (thinker_branch, talker_branch)
```

```python
import functools

import jax
import jax.numpy as jnp
from jax import lax
from jax.experimental import pallas as pl
from jax.experimental.pallas import tpu as pltpu
from jax.sharding import PartitionSpec as P

LANES = 128
TILE = 256
F32 = jnp.float32
BF16 = jnp.bfloat16


def slot_places(route):
    picks = route.shape[0] * route.shape[1]
    chosen = route.reshape(picks)
    order = jnp.arange(picks, dtype=jnp.int32)
    earlier = (chosen[:, None] == chosen[None, :]) & (order[None, :] < order[:, None])
    return (chosen, jnp.sum(earlier.astype(jnp.int32), axis=1))


def pack_rows(row_block, route, experts, capacity):
    chosen, places = slot_places(route)
    target = chosen * capacity + places
    copies = jnp.repeat(row_block, route.shape[1], axis=0)
    buffer = (
        jnp.zeros((experts * capacity, row_block.shape[1]), jnp.bfloat16).at[target].set(copies)
    )
    return (buffer, target)


def combine_rows(returned, target, weights):
    sessions, picks = weights.shape
    gathered = returned[target].astype(jnp.float32).reshape(sessions, picks, returned.shape[1])
    norm_weights = weights / jnp.sum(weights, axis=1, keepdims=True)
    return jnp.sum(gathered * norm_weights[:, :, None], axis=1).astype(jnp.bfloat16)


def swiglu(slab, gate_m, up_m, down_m):
    gate = jnp.dot(slab, gate_m, preferred_element_type=jnp.float32)
    upper = jnp.dot(slab, up_m, preferred_element_type=jnp.float32)
    hidden = (jax.nn.silu(gate) * upper).astype(jnp.bfloat16)
    return jnp.dot(hidden, down_m, preferred_element_type=jnp.float32)


def packed_on_device(
    thinker_rows,
    think_route,
    think_weight,
    think_gate,
    think_up,
    think_down,
    proj_weight,
    owner_map,
    talk_gain,
    talk_route,
    talk_weight,
    talk_gate,
    talk_up,
    talk_down,
):
    sessions = thinker_rows.shape[0]
    features = thinker_rows.shape[1]
    talk_features = talk_gate.shape[1]
    ep_count = lax.axis_size("ep")
    sess_count = lax.axis_size("sess")
    think_picks = think_route.shape[1]
    think_capacity = min(sessions, max(2, 2 * sessions * think_picks // ep_count))
    buffer, target = pack_rows(thinker_rows, think_route, ep_count, think_capacity)
    buffer = buffer.reshape(ep_count, think_capacity, features)
    gate_half = think_gate[0]
    up_half = think_up[0]
    down_half = think_down[0]
    paired = lax.all_gather(buffer, "sess", axis=1, tiled=True)
    arrived = lax.all_to_all(paired, "ep", split_axis=0, concat_axis=0, tiled=True)
    flattened = arrived.reshape(arrived.shape[0] * arrived.shape[1], features)
    result = swiglu(flattened, gate_half, up_half, down_half)
    partial_value = result.reshape(arrived.shape[0], arrived.shape[1], features)
    summed = lax.psum_scatter(partial_value, "sess", scatter_dimension=1, tiled=True).astype(
        jnp.bfloat16
    )
    returned = lax.all_to_all(summed, "ep", split_axis=0, concat_axis=0, tiled=True).reshape(
        ep_count * think_capacity, features
    )
    thinker_branch = combine_rows(returned, target, think_weight)
    projected = jnp.dot(
        lax.all_gather(thinker_branch, "sess", axis=0, tiled=True),
        proj_weight,
        preferred_element_type=jnp.float32,
    ).astype(jnp.bfloat16)
    block_rows = owner_map.shape[0]
    picker = (owner_map[:, None] == jnp.arange(block_rows, dtype=jnp.int32)[None, :]).astype(
        jnp.bfloat16
    )
    selected = jnp.dot(picker, projected, preferred_element_type=jnp.float32).astype(jnp.bfloat16)
    own_rows = lax.all_to_all(selected, "sess", split_axis=0, concat_axis=1, tiled=True).astype(
        jnp.float32
    )
    scale = lax.rsqrt(jnp.mean(own_rows * own_rows, axis=1, keepdims=True) + 1e-06)
    talk_rows = (own_rows * scale * talk_gain[None, :]).astype(jnp.bfloat16)
    talk_experts = ep_count * sess_count
    talk_picks = talk_route.shape[1]
    talk_capacity = min(sessions, max(2, 2 * sessions * talk_picks // talk_experts))
    talk_buffer, talk_target = pack_rows(talk_rows, talk_route, talk_experts, talk_capacity)
    talk_gate_m = talk_gate[0]
    talk_up_m = talk_up[0]
    talk_down_m = talk_down[0]
    sectioned_in = talk_buffer.reshape(talk_experts, talk_capacity, talk_features)
    portion = lax.all_to_all(sectioned_in, ("ep", "sess"), split_axis=0, concat_axis=0, tiled=True)
    flattened = portion.reshape(portion.shape[0] * portion.shape[1], talk_features)
    result = swiglu(flattened, talk_gate_m, talk_up_m, talk_down_m).astype(jnp.bfloat16)
    finished = result.reshape(portion.shape[0], portion.shape[1], talk_features)
    talk_returned = lax.all_to_all(
        finished, ("ep", "sess"), split_axis=0, concat_axis=0, tiled=True
    )
    talk_returned = talk_returned.reshape(talk_experts * talk_capacity, talk_features)
    talker_branch = combine_rows(talk_returned, talk_target, talk_weight)
    return (thinker_branch, talker_branch)


def dense_weights(route, weights, experts):
    rows, picks = route.shape
    lane = lax.broadcasted_iota(jnp.int32, (rows, LANES), 1)
    norm = weights / jnp.sum(weights, axis=1, keepdims=True)
    parts = jnp.zeros((rows, LANES), F32)
    for k in range(picks):
        value = norm[:, k : k + 1]
        high = value.astype(BF16).astype(F32)
        middle = (value - high).astype(BF16).astype(F32)
        low = value - high - middle
        chosen = route[:, k : k + 1]
        parts = parts + jnp.where(lane == chosen, high, 0.0)
        parts = parts + jnp.where(lane == chosen + experts, middle, 0.0)
        parts = parts + jnp.where(lane == chosen + 2 * experts, low, 0.0)
    return parts.astype(BF16)


class Place:
    def __init__(self, layers):
        self.layers = layers
        self.ep = lax.axis_index("ep")
        self.z = self.ep // 4
        self.x = (self.ep // 2) % 2
        self.c = self.ep % 2
        self.sibling = {"ep": self.ep + 1 - 2 * self.c}
        self.across = {"ep": self.ep + 2 - 4 * self.x}
        self.up = {"ep": self.ep + 4}
        self.down = {"ep": self.ep - 4}
        self.has_up = self.z < layers - 1
        self.has_down = self.z > 0


def remote(src, dst, send_sem, recv_sem, peer):
    return pltpu.make_async_remote_copy(
        src_ref=src,
        dst_ref=dst,
        send_sem=send_sem,
        recv_sem=recv_sem,
        device_id=peer,
        device_id_type=pl.DeviceIdType.MESH,
    )


def greet(place):
    barrier = pltpu.get_barrier_semaphore()

    def signal(peer):
        pl.semaphore_signal(barrier, inc=1, device_id=peer, device_id_type=pl.DeviceIdType.MESH)

    signal(place.sibling)
    signal(place.across)

    @pl.when(place.has_up)
    def _():
        signal(place.up)

    @pl.when(place.has_down)
    def _():
        signal(place.down)

    count = 2 + jnp.where(place.has_up, 1, 0) + jnp.where(place.has_down, 1, 0)
    pl.semaphore_wait(barrier, count)


def mixture_phase(place, features, gate_w, up_w, down_w, wait_weights, scratch):
    (held, hidden, scaled, partial, core_in, x_out, x_in, z_out, z_in,
     zs, zr, xs, xr, cs, cr, rs_cs, rs_cr, rs_xs, rs_xr, rs_zs, rs_zr) = scratch
    z, x, c, layers = place.z, place.x, place.c, place.layers
    rows = held.shape[3]
    group = 2 * layers * rows
    ff = gate_w.shape[1]

    def z_copy(way, step, block):
        slot = held.at[x, c, block]
        return remote(slot, slot, zs.at[way, step], zr.at[way, step], (place.up, place.down)[way])

    def x_copy(side, block):
        slot = held.at[side, c, block]
        return remote(slot, slot, xs.at[block], xr.at[block], place.across)

    def c_copy(side, core, block):
        slot = held.at[side, core, block]
        return remote(slot, slot, cs.at[side, block], cr.at[side, block], place.sibling)

    def fan(block):
        x_copy(x, block).start()
        c_copy(x, c, block).start()

    def arrivals(step, then):
        @pl.when(z - 1 - step >= 0)
        def _():
            then(0, z - 1 - step)

        @pl.when(z + 1 + step < layers)
        def _():
            then(1, z + 1 + step)

    def from_across(block):
        x_copy(1 - x, block).wait_recv()
        c_copy(1 - x, c, block).start()

    ahead = (place.has_up, place.has_down)
    for way in range(2):
        @pl.when(ahead[way])
        def _(way=way):
            z_copy(way, 0, z).start()

    fan(z)
    for step in range(layers - 1):
        def pass_on(way, block, step=step):
            z_copy(way, step, block).wait_recv()

            @pl.when(ahead[way])
            def _():
                z_copy(way, step + 1, block).start()

            fan(block)

        arrivals(step, pass_on)
        if step == 0:
            from_across(z)
        else:
            arrivals(step - 1, lambda way, block: from_across(block))

    def from_sibling(side):
        for block in range(layers):
            c_copy(side, 1 - c, block).wait_recv()

    def enter(side, which):
        def tile(i, carry):
            at = pl.ds(pl.multiple_of(i * width, width), width)
            slab = held[side, :, :, :, :features].reshape(group, features)
            gate = jnp.dot(slab, gate_w[:, at], preferred_element_type=F32)
            upper = jnp.dot(slab, up_w[:, at], preferred_element_type=F32)
            hidden[which, :, at] = (gate * (1.0 / (1.0 + jnp.exp(-gate))) * upper).astype(BF16)
            return carry

        width = TILE if ff % TILE == 0 else LANES
        lax.fori_loop(0, ff // width, tile, 0)
        parts = held[side, :, :, :, features:].reshape(group, LANES).astype(F32)
        lane = lax.broadcasted_iota(jnp.int32, (group, LANES), 1)
        experts = 4 * layers
        mine = (lane % experts == place.ep) & (lane < 3 * experts)
        scaled[which] = jnp.sum(jnp.where(mine, parts, 0.0), axis=1, keepdims=True)

    def leave(side, which):
        def tile(i, carry):
            at = pl.ds(pl.multiple_of(i * TILE, TILE), TILE)
            out = jnp.dot(hidden[which], down_w[:, at], preferred_element_type=F32)
            out = (out * scaled[which]).astype(BF16)
            partial[side, :, :, :, at] = out.reshape(2, layers, rows, TILE)
            return carry

        lax.fori_loop(0, features // TILE, tile, 0)

    from_sibling(x)
    wait_weights(0)
    enter(x, 0)
    arrivals(layers - 2, lambda way, block: from_across(block))
    from_sibling(1 - x)
    enter(1 - x, 1)
    wait_weights(1)
    leave(1 - x, 1)

    def core_sum(side, which):
        return remote(
            partial.at[side, 1 - c], core_in.at[which], rs_cs.at[which], rs_cr.at[which],
            place.sibling,
        )

    def x_sum(block):
        return remote(
            x_out.at[block], x_in.at[block], rs_xs.at[block], rs_xr.at[block], place.across
        )

    def z_sum(way, block):
        return remote(
            z_out.at[block], z_in.at[way, block], rs_zs.at[block], rs_zr.at[way, block],
            (place.up, place.down)[way],
        )

    def outward(then):
        for far in range(layers - 1, 0, -1):
            @pl.when(z + far < layers)
            def _(far=far):
                then(0, z + far)

            @pl.when(z - far >= 0)
            def _(far=far):
                then(1, z - far)

    core_sum(1 - x, 1).start()
    leave(x, 0)
    core_sum(x, 0).start()
    core_sum(1 - x, 1).wait_recv()

    def send_across(way, block):
        total = partial[1 - x, c, block].astype(F32) + core_in[1, block].astype(F32)
        x_out[block] = total.astype(BF16)
        x_sum(block).start()

    outward(send_across)
    send_across(0, z)
    core_sum(x, 0).wait_recv()

    def chip_total(block):
        total = partial[x, c, block].astype(F32) + core_in[0, block].astype(F32)
        x_sum(block).wait_recv()
        return total + x_in[block].astype(F32)

    behind = (place.has_down, place.has_up)

    def send_along(way, block):
        total = chip_total(block)

        @pl.when(behind[way])
        def _():
            z_sum(way, block).wait_recv()

        z_out[block] = (total + z_in[way, block].astype(F32)).astype(BF16)
        z_sum(way, block).start()

    outward(send_along)
    total = chip_total(z)
    for way in range(2):
        @pl.when(behind[way])
        def _(way=way):
            z_sum(way, z).wait_recv()

        total = total + z_in[way, z].astype(F32)

    def finish():
        for way in range(2):
            @pl.when(ahead[way])
            def _(way=way):
                z_copy(way, 0, z).wait_send()

        for step in range(layers - 1):
            def sent(way, block, step=step):
                @pl.when(ahead[way])
                def _():
                    z_copy(way, step + 1, block).wait_send()

            arrivals(step, sent)
        for block in range(layers):
            x_copy(x, block).wait_send()
            c_copy(x, c, block).wait_send()
            c_copy(1 - x, c, block).wait_send()
            x_sum(block).wait_send()
        core_sum(x, 0).wait_send()
        core_sum(1 - x, 1).wait_send()
        outward(lambda way, block: z_sum(way, block).wait_send())

    return total, finish


def clear_ends(place, z_in):
    for way, has in enumerate((place.has_down, place.has_up)):
        @pl.when(jnp.logical_not(has))
        def _(way=way):
            z_in[way] = jnp.zeros(z_in.shape[1:], z_in.dtype)


PHASE_REFS = 21


def step_kernel(
    layers,
    rows_ref, route_ref, weight_ref, gain_ref, owner_ref, talk_route_ref, talk_weight_ref,
    gate_hbm, up_hbm, down_hbm, proj_hbm, tgate_hbm, tup_hbm, tdown_hbm,
    think_out, talk_out,
    gate_v, up_v, down_v, proj_v, tgate_v, tup_v, tdown_v, load_sem,
    *phases,
):
    place = Place(layers)
    think, talk = phases[:PHASE_REFS], phases[PHASE_REFS:]
    pairs = (
        (gate_hbm.at[0], gate_v), (up_hbm.at[0], up_v), (down_hbm.at[0], down_v),
        (proj_hbm, proj_v),
        (tgate_hbm.at[0], tgate_v), (tup_hbm.at[0], tup_v), (tdown_hbm.at[0], tdown_v),
    )
    loads = [
        pltpu.make_async_copy(src, dst, load_sem.at[i]) for i, (src, dst) in enumerate(pairs)
    ]
    for load in loads:
        load.start()
    experts = 4 * layers
    features = rows_ref.shape[1]
    talk_features = gain_ref.shape[1]
    z, x, c = place.z, place.x, place.c
    held, talk_held = think[0], talk[0]
    held[x, c, z, :, :features] = rows_ref[...]
    held[x, c, z, :, features:] = dense_weights(route_ref[...], weight_ref[...], experts)
    talk_held[x, c, z, :, talk_features:] = dense_weights(
        talk_route_ref[...], talk_weight_ref[...], experts
    )
    clear_ends(place, think[8])
    clear_ends(place, talk[8])
    greet(place)

    def wait_think(stage):
        for load in (loads[:2], loads[2:3])[stage]:
            load.wait()

    def wait_talk(stage):
        for load in (loads[4:6], loads[6:7])[stage]:
            load.wait()

    total, finish_think = mixture_phase(place, features, gate_v, up_v, down_v, wait_think, think)
    branch = total.astype(BF16)
    think_out[...] = branch
    loads[3].wait()
    projected = jnp.dot(branch, proj_v[...], preferred_element_type=F32).astype(BF16)
    count = owner_ref.shape[0]
    spot = lax.broadcasted_iota(jnp.int32, (count, count), 1)
    picker = jnp.where(owner_ref[...] == spot, 1.0, 0.0).astype(BF16)
    own_rows = jnp.dot(picker, projected, preferred_element_type=F32)
    scale = lax.rsqrt(jnp.mean(own_rows * own_rows, axis=1, keepdims=True) + 1e-06)
    talk_held[x, c, z, :, :talk_features] = (own_rows * scale * gain_ref[...]).astype(BF16)
    total, finish_talk = mixture_phase(
        place, talk_features, tgate_v, tup_v, tdown_v, wait_talk, talk
    )
    talk_out[...] = total.astype(BF16)
    finish_think()
    finish_talk()


def phase_scratch(layers, rows, features, ff):
    group = 2 * layers * rows
    dma = pltpu.SemaphoreType.DMA
    block = (layers, rows, features)
    return [
        pltpu.VMEM((2, 2, layers, rows, features + LANES), BF16),
        pltpu.VMEM((2, group, ff), BF16),
        pltpu.VMEM((2, group, 1), F32),
        pltpu.VMEM((2, 2) + block, BF16),
        pltpu.VMEM((2,) + block, BF16),
        pltpu.VMEM(block, BF16),
        pltpu.VMEM(block, BF16),
        pltpu.VMEM(block, BF16),
        pltpu.VMEM((2,) + block, BF16),
        dma((2, layers)), dma((2, layers)),
        dma((layers,)), dma((layers,)),
        dma((2, layers)), dma((2, layers)),
        dma((2,)), dma((2,)),
        dma((layers,)), dma((layers,)),
        dma((layers,)), dma((2, layers)),
    ]


def dense_on_device(
    thinker_rows, think_route, think_weight, think_gate, think_up, think_down, proj_weight,
    owner_map, talk_gain, talk_route, talk_weight, talk_gate, talk_up, talk_down,
):
    layers = lax.axis_size("ep") // 4
    rows, features = thinker_rows.shape
    talk_features, talk_ff = talk_gate.shape[1:]
    ff = think_gate.shape[2]
    vmem = pl.BlockSpec(memory_space=pltpu.VMEM)
    hbm = pl.BlockSpec(memory_space=pl.ANY)
    weights = (think_gate, think_up, think_down, proj_weight, talk_gate, talk_up, talk_down)
    sizes = [w.shape[-2:] for w in weights]
    all_rows = 4 * layers * rows
    return pl.pallas_call(
        functools.partial(step_kernel, layers),
        out_shape=(
            jax.ShapeDtypeStruct((rows, features), BF16),
            jax.ShapeDtypeStruct((rows, talk_features), BF16),
        ),
        in_specs=[vmem] * 7 + [hbm] * 7,
        out_specs=(vmem, vmem),
        scratch_shapes=[pltpu.VMEM(size, BF16) for size in sizes]
        + [pltpu.SemaphoreType.DMA((len(sizes),))]
        + phase_scratch(layers, rows, features, ff)
        + phase_scratch(layers, rows, talk_features, talk_ff),
        compiler_params=pltpu.CompilerParams(
            collective_id=0, has_side_effects=True, vmem_limit_bytes=56 * 1024 * 1024
        ),
        cost_estimate=pl.CostEstimate(
            flops=6 * all_rows * (features * ff + talk_features * talk_ff),
            bytes_accessed=2 * sum(a * b for a, b in sizes),
            transcendentals=all_rows * (ff + talk_ff),
        ),
    )(
        thinker_rows, think_route, think_weight, talk_gain[None, :], owner_map[:, None],
        talk_route, talk_weight, *weights,
    )


def on_device(*arguments):
    rows, picks = arguments[1].shape
    talk_rows, talk_picks = arguments[9].shape
    ep_count = lax.axis_size("ep")
    whole = lax.axis_size("sess") == 1 and ep_count % 4 == 0 and 3 * ep_count <= LANES
    if whole and ep_count >= 8 and 2 * picks >= ep_count and arguments[0].shape[1] % TILE == 0:
        return dense_on_device(*arguments)
    return packed_on_device(*arguments)


def solution(mesh):
    return jax.shard_map(
        on_device,
        mesh=mesh,
        in_specs=(
            P(("grp", "ep", "sess"), None),
            P(("grp", "ep", "sess"), None),
            P(("grp", "ep", "sess"), None),
            P("ep", None, "sess"),
            P("ep", None, "sess"),
            P("ep", "sess", None),
            P(None, "sess"),
            P(("grp", "ep")),
            P(),
            P(("grp", "ep", "sess"), None),
            P(("grp", "ep", "sess"), None),
            P(("ep", "sess"), None, None),
            P(("ep", "sess"), None, None),
            P(("ep", "sess"), None, None),
        ),
        out_specs=(P(("grp", "ep", "sess"), None), P(("grp", "ep", "sess"), None)),
        check_vma=False,
    )
```

```python
import functools

import jax
import jax.numpy as jnp
from jax import lax
from jax.experimental import pallas as pl
from jax.experimental.pallas import tpu as pltpu
from jax.sharding import PartitionSpec as P

LANES = 128
TILE = 256
F32 = jnp.float32
BF16 = jnp.bfloat16


def slot_places(route):
    picks = route.shape[0] * route.shape[1]
    chosen = route.reshape(picks)
    order = jnp.arange(picks, dtype=jnp.int32)
    earlier = (chosen[:, None] == chosen[None, :]) & (order[None, :] < order[:, None])
    return (chosen, jnp.sum(earlier.astype(jnp.int32), axis=1))


def pack_rows(row_block, route, experts, capacity):
    chosen, places = slot_places(route)
    target = chosen * capacity + places
    copies = jnp.repeat(row_block, route.shape[1], axis=0)
    buffer = (
        jnp.zeros((experts * capacity, row_block.shape[1]), jnp.bfloat16).at[target].set(copies)
    )
    return (buffer, target)


def combine_rows(returned, target, weights):
    sessions, picks = weights.shape
    gathered = returned[target].astype(jnp.float32).reshape(sessions, picks, returned.shape[1])
    norm_weights = weights / jnp.sum(weights, axis=1, keepdims=True)
    return jnp.sum(gathered * norm_weights[:, :, None], axis=1).astype(jnp.bfloat16)


def swiglu(slab, gate_m, up_m, down_m):
    gate = jnp.dot(slab, gate_m, preferred_element_type=jnp.float32)
    upper = jnp.dot(slab, up_m, preferred_element_type=jnp.float32)
    hidden = (jax.nn.silu(gate) * upper).astype(jnp.bfloat16)
    return jnp.dot(hidden, down_m, preferred_element_type=jnp.float32)


def packed_on_device(
    thinker_rows,
    think_route,
    think_weight,
    think_gate,
    think_up,
    think_down,
    proj_weight,
    owner_map,
    talk_gain,
    talk_route,
    talk_weight,
    talk_gate,
    talk_up,
    talk_down,
):
    sessions = thinker_rows.shape[0]
    features = thinker_rows.shape[1]
    talk_features = talk_gate.shape[1]
    ep_count = lax.axis_size("ep")
    sess_count = lax.axis_size("sess")
    think_picks = think_route.shape[1]
    think_capacity = min(sessions, max(2, 2 * sessions * think_picks // ep_count))
    buffer, target = pack_rows(thinker_rows, think_route, ep_count, think_capacity)
    buffer = buffer.reshape(ep_count, think_capacity, features)
    gate_half = think_gate[0]
    up_half = think_up[0]
    down_half = think_down[0]
    paired = lax.all_gather(buffer, "sess", axis=1, tiled=True)
    arrived = lax.all_to_all(paired, "ep", split_axis=0, concat_axis=0, tiled=True)
    flattened = arrived.reshape(arrived.shape[0] * arrived.shape[1], features)
    result = swiglu(flattened, gate_half, up_half, down_half)
    partial_value = result.reshape(arrived.shape[0], arrived.shape[1], features)
    summed = lax.psum_scatter(partial_value, "sess", scatter_dimension=1, tiled=True).astype(
        jnp.bfloat16
    )
    returned = lax.all_to_all(summed, "ep", split_axis=0, concat_axis=0, tiled=True).reshape(
        ep_count * think_capacity, features
    )
    thinker_branch = combine_rows(returned, target, think_weight)
    projected = jnp.dot(
        lax.all_gather(thinker_branch, "sess", axis=0, tiled=True),
        proj_weight,
        preferred_element_type=jnp.float32,
    ).astype(jnp.bfloat16)
    block_rows = owner_map.shape[0]
    picker = (owner_map[:, None] == jnp.arange(block_rows, dtype=jnp.int32)[None, :]).astype(
        jnp.bfloat16
    )
    selected = jnp.dot(picker, projected, preferred_element_type=jnp.float32).astype(jnp.bfloat16)
    own_rows = lax.all_to_all(selected, "sess", split_axis=0, concat_axis=1, tiled=True).astype(
        jnp.float32
    )
    scale = lax.rsqrt(jnp.mean(own_rows * own_rows, axis=1, keepdims=True) + 1e-06)
    talk_rows = (own_rows * scale * talk_gain[None, :]).astype(jnp.bfloat16)
    talk_experts = ep_count * sess_count
    talk_picks = talk_route.shape[1]
    talk_capacity = min(sessions, max(2, 2 * sessions * talk_picks // talk_experts))
    talk_buffer, talk_target = pack_rows(talk_rows, talk_route, talk_experts, talk_capacity)
    talk_gate_m = talk_gate[0]
    talk_up_m = talk_up[0]
    talk_down_m = talk_down[0]
    sectioned_in = talk_buffer.reshape(talk_experts, talk_capacity, talk_features)
    portion = lax.all_to_all(sectioned_in, ("ep", "sess"), split_axis=0, concat_axis=0, tiled=True)
    flattened = portion.reshape(portion.shape[0] * portion.shape[1], talk_features)
    result = swiglu(flattened, talk_gate_m, talk_up_m, talk_down_m).astype(jnp.bfloat16)
    finished = result.reshape(portion.shape[0], portion.shape[1], talk_features)
    talk_returned = lax.all_to_all(
        finished, ("ep", "sess"), split_axis=0, concat_axis=0, tiled=True
    )
    talk_returned = talk_returned.reshape(talk_experts * talk_capacity, talk_features)
    talker_branch = combine_rows(talk_returned, talk_target, talk_weight)
    return (thinker_branch, talker_branch)


def dense_weights(route, weights, experts):
    picks, rows = route.shape
    spot = lax.broadcasted_iota(jnp.int32, (LANES, rows), 0)
    norm = weights / jnp.sum(weights, axis=0, keepdims=True)
    parts = jnp.zeros((LANES, rows), F32)
    for k in range(picks):
        value = norm[k : k + 1]
        high = value.astype(BF16).astype(F32)
        middle = (value - high).astype(BF16).astype(F32)
        low = value - high - middle
        chosen = route[k : k + 1]
        parts = parts + jnp.where(spot == chosen, high, 0.0)
        parts = parts + jnp.where(spot == chosen + experts, middle, 0.0)
        parts = parts + jnp.where(spot == chosen + 2 * experts, low, 0.0)
    down = lax.broadcasted_iota(jnp.int32, (rows, rows), 0)
    along = lax.broadcasted_iota(jnp.int32, (rows, rows), 1)
    turned = lax.dot_general(
        jnp.where(down == along, 1.0, 0.0).astype(BF16), parts.astype(BF16),
        (((1,), (1,)), ((), ())), preferred_element_type=F32,
    )
    return turned.astype(BF16)


class Place:
    def __init__(self, layers):
        self.layers = layers
        self.ep = lax.axis_index("ep")
        self.z = self.ep // 4
        self.x = (self.ep // 2) % 2
        self.c = self.ep % 2
        self.sibling = {"ep": self.ep + 1 - 2 * self.c}
        self.across = {"ep": self.ep + 2 - 4 * self.x}
        self.up = {"ep": self.ep + 4}
        self.down = {"ep": self.ep - 4}
        self.has_up = self.z < layers - 1
        self.has_down = self.z > 0


def remote(src, dst, send_sem, recv_sem, peer):
    return pltpu.make_async_remote_copy(
        src_ref=src,
        dst_ref=dst,
        send_sem=send_sem,
        recv_sem=recv_sem,
        device_id=peer,
        device_id_type=pl.DeviceIdType.MESH,
    )


def greet(place):
    barrier = pltpu.get_barrier_semaphore()

    def signal(peer):
        pl.semaphore_signal(barrier, inc=1, device_id=peer, device_id_type=pl.DeviceIdType.MESH)

    signal(place.sibling)
    signal(place.across)

    @pl.when(place.has_up)
    def _():
        signal(place.up)

    @pl.when(place.has_down)
    def _():
        signal(place.down)

    count = 2 + jnp.where(place.has_up, 1, 0) + jnp.where(place.has_down, 1, 0)
    pl.semaphore_wait(barrier, count)


class Mixture:
    def __init__(self, place, features, weights, scratch):
        self.place, self.features, self.weights = place, features, weights
        (self.held, self.hidden, self.scaled, self.partial, self.core_in, self.x_out,
         self.x_in, self.z_out, self.z_in,
         self.zs, self.zr, self.xs, self.xr, self.cs, self.cr,
         self.rs_cs, self.rs_cr, self.rs_xs, self.rs_xr, self.rs_zs, self.rs_zr) = scratch
        self.layers = place.layers
        self.ahead = (place.has_up, place.has_down)
        self.behind = (place.has_down, place.has_up)
        self.peers = (place.up, place.down)

    def z_copy(self, way, step, block):
        slot = self.held.at[self.place.x, self.place.c, block]
        return remote(slot, slot, self.zs.at[way, step], self.zr.at[way, step], self.peers[way])

    def x_copy(self, side, block):
        slot = self.held.at[side, self.place.c, block]
        return remote(slot, slot, self.xs.at[block], self.xr.at[block], self.place.across)

    def c_copy(self, side, core, block):
        slot = self.held.at[side, core, block]
        return remote(
            slot, slot, self.cs.at[side, block], self.cr.at[side, block], self.place.sibling
        )

    def fan(self, block):
        self.x_copy(self.place.x, block).start()
        self.c_copy(self.place.x, self.place.c, block).start()

    def arrivals(self, step, then):
        z = self.place.z

        @pl.when(z - 1 - step >= 0)
        def _():
            then(0, z - 1 - step)

        @pl.when(z + 1 + step < self.layers)
        def _():
            then(1, z + 1 + step)

    def from_across(self, block):
        side = 1 - self.place.x
        self.x_copy(side, block).wait_recv()
        self.c_copy(side, self.place.c, block).start()

    def gather_start(self):
        z = self.place.z
        for way in range(2):
            @pl.when(self.ahead[way])
            def _(way=way):
                self.z_copy(way, 0, z).start()

        self.fan(z)

    def gather_step(self, step):
        def pass_on(way, block):
            self.z_copy(way, step, block).wait_recv()

            @pl.when(self.ahead[way])
            def _():
                self.z_copy(way, step + 1, block).start()

            self.fan(block)

        if step < self.layers - 1:
            self.arrivals(step, pass_on)
        if step == 0:
            self.from_across(self.place.z)
        else:
            self.arrivals(step - 1, lambda way, block: self.from_across(block))

    def gather_end(self):
        for side in range(2):
            for block in range(self.layers):
                self.c_copy(side, 1 - self.place.c, block).wait_recv()

    def enter(self, first, last):
        gate_w, up_w, _ = self.weights
        group = self.hidden.shape[0]
        ff = gate_w.shape[1]
        width = TILE if ff % TILE == 0 else LANES

        def tile(i, carry):
            at = pl.ds(pl.multiple_of(i * width, width), width)
            slab = self.held[:, :, :, :, : self.features].reshape(group, self.features)
            gate = jnp.dot(slab, gate_w[:, at], preferred_element_type=F32)
            upper = jnp.dot(slab, up_w[:, at], preferred_element_type=F32)
            self.hidden[:, at] = (gate * (1.0 / (1.0 + jnp.exp(-gate))) * upper).astype(BF16)
            return carry

        tiles = ff // width
        lax.fori_loop(int(first * tiles), int(last * tiles), tile, 0)

    def weigh(self):
        group = self.hidden.shape[0]
        parts = self.held[:, :, :, :, self.features :].reshape(group, LANES).astype(F32)
        lane = lax.broadcasted_iota(jnp.int32, (group, LANES), 1)
        experts = 4 * self.layers
        mine = (lane % experts == self.place.ep) & (lane < 3 * experts)
        self.scaled[...] = jnp.sum(jnp.where(mine, parts, 0.0), axis=1, keepdims=True)

    def leave(self, first, last):
        down_w = self.weights[2]
        rows = self.held.shape[3]

        def tile(i, carry):
            at = pl.ds(pl.multiple_of(i * TILE, TILE), TILE)
            out = jnp.dot(self.hidden[...], down_w[:, at], preferred_element_type=F32)
            out = (out * self.scaled[...]).astype(BF16)
            self.partial[:, :, :, :, at] = out.reshape(2, 2, self.layers, rows, TILE)
            return carry

        tiles = self.features // TILE
        lax.fori_loop(int(first * tiles), int(last * tiles), tile, 0)

    def core_sum(self, side):
        return remote(
            self.partial.at[side, 1 - self.place.c], self.core_in.at[side],
            self.rs_cs.at[side], self.rs_cr.at[side], self.place.sibling,
        )

    def x_sum(self, block):
        return remote(
            self.x_out.at[block], self.x_in.at[block], self.rs_xs.at[block],
            self.rs_xr.at[block], self.place.across,
        )

    def z_sum(self, way, block):
        return remote(
            self.z_out.at[block], self.z_in.at[way, block], self.rs_zs.at[block],
            self.rs_zr.at[way, block], self.peers[way],
        )

    def outward(self, then, far):
        z = self.place.z

        @pl.when(z + far < self.layers)
        def _():
            then(0, z + far)

        @pl.when(z - far >= 0)
        def _():
            then(1, z - far)

    def sum_start(self):
        self.core_sum(1 - self.place.x).start()
        self.core_sum(self.place.x).start()

    def sum_across(self):
        x, c = self.place.x, self.place.c
        self.core_sum(1 - x).wait_recv()

        def send(way, block):
            total = self.partial[1 - x, c, block].astype(F32)
            total = total + self.core_in[1 - x, block].astype(F32)
            self.x_out[block] = total.astype(BF16)
            self.x_sum(block).start()

        for far in range(self.layers - 1, 0, -1):
            self.outward(send, far)
        send(0, self.place.z)
        self.core_sum(x).wait_recv()

    def chip_total(self, block):
        x, c = self.place.x, self.place.c
        total = self.partial[x, c, block].astype(F32) + self.core_in[x, block].astype(F32)
        self.x_sum(block).wait_recv()
        return total + self.x_in[block].astype(F32)

    def sum_along(self, far):
        def send(way, block):
            total = self.chip_total(block)

            @pl.when(self.behind[way])
            def _():
                self.z_sum(way, block).wait_recv()

            self.z_out[block] = (total + self.z_in[way, block].astype(F32)).astype(BF16)
            self.z_sum(way, block).start()

        self.outward(send, far)

    def sum_end(self):
        z = self.place.z
        total = self.chip_total(z)
        for way in range(2):
            @pl.when(self.behind[way])
            def _(way=way):
                self.z_sum(way, z).wait_recv()

            total = total + self.z_in[way, z].astype(F32)
        return total

    def finish(self):
        x, c, z = self.place.x, self.place.c, self.place.z
        for way in range(2):
            @pl.when(self.ahead[way])
            def _(way=way):
                self.z_copy(way, 0, z).wait_send()

        for step in range(self.layers - 1):
            def sent(way, block, step=step):
                @pl.when(self.ahead[way])
                def _():
                    self.z_copy(way, step + 1, block).wait_send()

            self.arrivals(step, sent)
        for block in range(self.layers):
            self.x_copy(x, block).wait_send()
            self.c_copy(x, c, block).wait_send()
            self.c_copy(1 - x, c, block).wait_send()
            self.x_sum(block).wait_send()
        for side in range(2):
            self.core_sum(side).wait_send()
        for far in range(self.layers - 1, 0, -1):
            self.outward(lambda way, block: self.z_sum(way, block).wait_send(), far)


def run_halves(first, second, wait_weights):
    layers = first.layers
    first.gather_start()
    second.gather_start()
    for step in range(layers):
        first.gather_step(step)
    second.gather_step(0)
    first.gather_end()
    wait_weights(0)
    first.weigh()
    pieces = layers - 1
    for piece in range(pieces):
        first.enter(piece / pieces, (piece + 1) / pieces)
        second.gather_step(piece + 1)
    wait_weights(1)
    first.leave(0, 1)
    first.sum_start()
    second.gather_end()
    second.weigh()
    second.enter(0, 0.34)
    first.sum_across()
    second.enter(0.34, 1)
    for far in range(layers - 1, 0, -1):
        first.sum_along(far)
        done = layers - 1 - far
        second.leave(done / pieces, (done + 1) / pieces)
    second.sum_start()
    top = first.sum_end()
    second.sum_across()
    for far in range(layers - 1, 0, -1):
        second.sum_along(far)
    return top, second.sum_end()


def clear_ends(place, z_in):
    for way, has in enumerate((place.has_down, place.has_up)):
        @pl.when(jnp.logical_not(has))
        def _(way=way):
            z_in[way] = jnp.zeros(z_in.shape[1:], z_in.dtype)


PHASE_REFS = 21


def step_kernel(
    layers,
    rows_ref, route_ref, weight_ref, gain_ref, owner_ref, talk_route_ref, talk_weight_ref,
    gate_hbm, up_hbm, down_hbm, proj_hbm, tgate_hbm, tup_hbm, tdown_hbm,
    think_out, talk_out,
    gate_v, up_v, down_v, proj_v, tgate_v, tup_v, tdown_v, load_sem,
    *phases,
):
    place = Place(layers)
    scratches = [phases[i : i + PHASE_REFS] for i in range(0, len(phases), PHASE_REFS)]
    pairs = (
        (gate_hbm.at[0], gate_v), (up_hbm.at[0], up_v), (down_hbm.at[0], down_v),
        (proj_hbm, proj_v),
        (tgate_hbm.at[0], tgate_v), (tup_hbm.at[0], tup_v), (tdown_hbm.at[0], tdown_v),
    )
    loads = [
        pltpu.make_async_copy(src, dst, load_sem.at[i]) for i, (src, dst) in enumerate(pairs)
    ]
    experts = 4 * layers
    rows, features = rows_ref.shape
    half = rows // 2
    talk_features = gain_ref.shape[1]
    z, x, c = place.z, place.x, place.c
    thinks = [Mixture(place, features, (gate_v, up_v, down_v), s) for s in scratches[:2]]
    talks = [Mixture(place, talk_features, (tgate_v, tup_v, tdown_v), s) for s in scratches[2:]]
    cuts = (pl.ds(0, half), pl.ds(half, half))
    think_parts = dense_weights(route_ref[...], weight_ref[...], experts)
    talk_parts = dense_weights(talk_route_ref[...], talk_weight_ref[...], experts)
    for i, cut in enumerate(cuts):
        own = slice(i * half, (i + 1) * half)
        thinks[i].held[x, c, z, :, :features] = rows_ref[cut, :]
        thinks[i].held[x, c, z, :, features:] = think_parts[own]
        talks[i].held[x, c, z, :, talk_features:] = talk_parts[own]
        clear_ends(place, thinks[i].z_in)
        clear_ends(place, talks[i].z_in)
    greet(place)
    for load in loads:
        load.start()

    def wait_think(stage):
        for load in (loads[:2], loads[2:3])[stage]:
            load.wait()

    def wait_talk(stage):
        for load in (loads[4:6], loads[6:7])[stage]:
            load.wait()

    totals = run_halves(*thinks, wait_think)
    branch = jnp.concatenate(totals, axis=0).astype(BF16)
    think_out[...] = branch
    loads[3].wait()
    projected = jnp.dot(branch, proj_v[...], preferred_element_type=F32).astype(BF16)
    count = owner_ref.shape[1]
    spot = lax.broadcasted_iota(jnp.int32, (count, count), 0)
    picker = jnp.where(owner_ref[...] == spot, 1.0, 0.0).astype(BF16)
    own_rows = lax.dot_general(
        picker, projected, (((0,), (0,)), ((), ())), preferred_element_type=F32
    )
    scale = lax.rsqrt(jnp.mean(own_rows * own_rows, axis=1, keepdims=True) + 1e-06)
    talk_rows = (own_rows * scale * gain_ref[...]).astype(BF16)
    for i in range(2):
        talks[i].held[x, c, z, :, :talk_features] = talk_rows[i * half : (i + 1) * half]
    totals = run_halves(*talks, wait_talk)
    talk_out[...] = jnp.concatenate(totals, axis=0).astype(BF16)
    for mixture in thinks + talks:
        mixture.finish()


def hand_over(think_in, talk_in, think_out, talk_out, sem):
    copies = [
        pltpu.make_async_copy(src, dst, sem.at[i])
        for i, (src, dst) in enumerate(((think_in, think_out), (talk_in, talk_out)))
    ]
    for copy in copies:
        copy.start()
    for copy in copies:
        copy.wait()


def phase_scratch(layers, rows, features, ff):
    group = 4 * layers * rows
    dma = pltpu.SemaphoreType.DMA
    block = (layers, rows, features)
    return [
        pltpu.VMEM((2, 2, layers, rows, features + LANES), BF16),
        pltpu.VMEM((group, ff), BF16),
        pltpu.VMEM((group, 1), F32),
        pltpu.VMEM((2, 2) + block, BF16),
        pltpu.VMEM((2,) + block, BF16),
        pltpu.VMEM(block, BF16),
        pltpu.VMEM(block, BF16),
        pltpu.VMEM(block, BF16),
        pltpu.VMEM((2,) + block, BF16),
        dma((2, layers)), dma((2, layers)),
        dma((layers,)), dma((layers,)),
        dma((2, layers)), dma((2, layers)),
        dma((2,)), dma((2,)),
        dma((layers,)), dma((layers,)),
        dma((layers,)), dma((2, layers)),
    ]


def dense_on_device(
    thinker_rows, think_route, think_weight, think_gate, think_up, think_down, proj_weight,
    owner_map, talk_gain, talk_route, talk_weight, talk_gate, talk_up, talk_down,
):
    layers = lax.axis_size("ep") // 4
    rows, features = thinker_rows.shape
    talk_features, talk_ff = talk_gate.shape[1:]
    ff = think_gate.shape[2]
    vmem = pl.BlockSpec(memory_space=pltpu.VMEM)
    hbm = pl.BlockSpec(memory_space=pl.ANY)
    weights = (think_gate, think_up, think_down, proj_weight, talk_gate, talk_up, talk_down)
    sizes = [w.shape[-2:] for w in weights]
    all_rows = 4 * layers * rows
    outs = (
        jax.ShapeDtypeStruct((rows, features), BF16),
        jax.ShapeDtypeStruct((rows, talk_features), BF16),
    )
    branches = pl.pallas_call(
        functools.partial(step_kernel, layers),
        out_shape=outs,
        in_specs=[vmem] * 7 + [hbm] * 7,
        out_specs=(vmem, vmem),
        scratch_shapes=[pltpu.VMEM(size, BF16) for size in sizes]
        + [pltpu.SemaphoreType.DMA((len(sizes),))]
        + 2 * phase_scratch(layers, rows // 2, features, ff)
        + 2 * phase_scratch(layers, rows // 2, talk_features, talk_ff),
        compiler_params=pltpu.CompilerParams(
            collective_id=0, has_side_effects=True, vmem_limit_bytes=56 * 1024 * 1024
        ),
        cost_estimate=pl.CostEstimate(
            flops=6 * all_rows * (features * ff + talk_features * talk_ff),
            bytes_accessed=2 * sum(a * b for a, b in sizes),
            transcendentals=all_rows * (ff + talk_ff),
        ),
    )(
        thinker_rows, think_route.T, think_weight.T, talk_gain[None, :], owner_map[None, :],
        talk_route.T, talk_weight.T, *weights,
    )
    return pl.pallas_call(
        hand_over,
        out_shape=outs,
        in_specs=[hbm, hbm],
        out_specs=(hbm, hbm),
        scratch_shapes=[pltpu.SemaphoreType.DMA((2,))],
    )(*branches)


def on_device(*arguments):
    rows, picks = arguments[1].shape
    ep_count = lax.axis_size("ep")
    whole = lax.axis_size("sess") == 1 and ep_count % 4 == 0 and 3 * ep_count <= LANES
    whole = whole and ep_count >= 8 and rows % 32 == 0 and 2 * picks >= ep_count
    if whole and arguments[0].shape[1] % TILE == 0 and arguments[8].shape[0] % TILE == 0:
        return dense_on_device(*arguments)
    return packed_on_device(*arguments)


def solution(mesh):
    return jax.shard_map(
        on_device,
        mesh=mesh,
        in_specs=(
            P(("grp", "ep", "sess"), None),
            P(("grp", "ep", "sess"), None),
            P(("grp", "ep", "sess"), None),
            P("ep", None, "sess"),
            P("ep", None, "sess"),
            P("ep", "sess", None),
            P(None, "sess"),
            P(("grp", "ep")),
            P(),
            P(("grp", "ep", "sess"), None),
            P(("grp", "ep", "sess"), None),
            P(("ep", "sess"), None, None),
            P(("ep", "sess"), None, None),
            P(("ep", "sess"), None, None),
        ),
        out_specs=(P(("grp", "ep", "sess"), None), P(("grp", "ep", "sess"), None)),
        check_vma=False,
    )
```

```python
import functools

import jax
import jax.numpy as jnp
from jax import lax
from jax.experimental import pallas as pl
from jax.experimental.pallas import tpu as pltpu
from jax.sharding import PartitionSpec as P

LANES = 128
TILE = 256
F32 = jnp.float32
BF16 = jnp.bfloat16


def slot_places(route):
    picks = route.shape[0] * route.shape[1]
    chosen = route.reshape(picks)
    order = jnp.arange(picks, dtype=jnp.int32)
    earlier = (chosen[:, None] == chosen[None, :]) & (order[None, :] < order[:, None])
    return (chosen, jnp.sum(earlier.astype(jnp.int32), axis=1))


def pack_rows(row_block, route, experts, capacity):
    chosen, places = slot_places(route)
    target = chosen * capacity + places
    copies = jnp.repeat(row_block, route.shape[1], axis=0)
    buffer = (
        jnp.zeros((experts * capacity, row_block.shape[1]), jnp.bfloat16).at[target].set(copies)
    )
    return (buffer, target)


def combine_rows(returned, target, weights):
    sessions, picks = weights.shape
    gathered = returned[target].astype(jnp.float32).reshape(sessions, picks, returned.shape[1])
    norm_weights = weights / jnp.sum(weights, axis=1, keepdims=True)
    return jnp.sum(gathered * norm_weights[:, :, None], axis=1).astype(jnp.bfloat16)


def swiglu(slab, gate_m, up_m, down_m):
    gate = jnp.dot(slab, gate_m, preferred_element_type=jnp.float32)
    upper = jnp.dot(slab, up_m, preferred_element_type=jnp.float32)
    hidden = (jax.nn.silu(gate) * upper).astype(jnp.bfloat16)
    return jnp.dot(hidden, down_m, preferred_element_type=jnp.float32)


def packed_on_device(
    thinker_rows,
    think_route,
    think_weight,
    think_gate,
    think_up,
    think_down,
    proj_weight,
    owner_map,
    talk_gain,
    talk_route,
    talk_weight,
    talk_gate,
    talk_up,
    talk_down,
):
    sessions = thinker_rows.shape[0]
    features = thinker_rows.shape[1]
    talk_features = talk_gate.shape[1]
    ep_count = lax.axis_size("ep")
    sess_count = lax.axis_size("sess")
    think_picks = think_route.shape[1]
    think_capacity = min(sessions, max(2, 2 * sessions * think_picks // ep_count))
    buffer, target = pack_rows(thinker_rows, think_route, ep_count, think_capacity)
    buffer = buffer.reshape(ep_count, think_capacity, features)
    gate_half = think_gate[0]
    up_half = think_up[0]
    down_half = think_down[0]
    paired = lax.all_gather(buffer, "sess", axis=1, tiled=True)
    arrived = lax.all_to_all(paired, "ep", split_axis=0, concat_axis=0, tiled=True)
    flattened = arrived.reshape(arrived.shape[0] * arrived.shape[1], features)
    result = swiglu(flattened, gate_half, up_half, down_half)
    partial_value = result.reshape(arrived.shape[0], arrived.shape[1], features)
    summed = lax.psum_scatter(partial_value, "sess", scatter_dimension=1, tiled=True).astype(
        jnp.bfloat16
    )
    returned = lax.all_to_all(summed, "ep", split_axis=0, concat_axis=0, tiled=True).reshape(
        ep_count * think_capacity, features
    )
    thinker_branch = combine_rows(returned, target, think_weight)
    projected = jnp.dot(
        lax.all_gather(thinker_branch, "sess", axis=0, tiled=True),
        proj_weight,
        preferred_element_type=jnp.float32,
    ).astype(jnp.bfloat16)
    block_rows = owner_map.shape[0]
    picker = (owner_map[:, None] == jnp.arange(block_rows, dtype=jnp.int32)[None, :]).astype(
        jnp.bfloat16
    )
    selected = jnp.dot(picker, projected, preferred_element_type=jnp.float32).astype(jnp.bfloat16)
    own_rows = lax.all_to_all(selected, "sess", split_axis=0, concat_axis=1, tiled=True).astype(
        jnp.float32
    )
    scale = lax.rsqrt(jnp.mean(own_rows * own_rows, axis=1, keepdims=True) + 1e-06)
    talk_rows = (own_rows * scale * talk_gain[None, :]).astype(jnp.bfloat16)
    talk_experts = ep_count * sess_count
    talk_picks = talk_route.shape[1]
    talk_capacity = min(sessions, max(2, 2 * sessions * talk_picks // talk_experts))
    talk_buffer, talk_target = pack_rows(talk_rows, talk_route, talk_experts, talk_capacity)
    talk_gate_m = talk_gate[0]
    talk_up_m = talk_up[0]
    talk_down_m = talk_down[0]
    sectioned_in = talk_buffer.reshape(talk_experts, talk_capacity, talk_features)
    portion = lax.all_to_all(sectioned_in, ("ep", "sess"), split_axis=0, concat_axis=0, tiled=True)
    flattened = portion.reshape(portion.shape[0] * portion.shape[1], talk_features)
    result = swiglu(flattened, talk_gate_m, talk_up_m, talk_down_m).astype(jnp.bfloat16)
    finished = result.reshape(portion.shape[0], portion.shape[1], talk_features)
    talk_returned = lax.all_to_all(
        finished, ("ep", "sess"), split_axis=0, concat_axis=0, tiled=True
    )
    talk_returned = talk_returned.reshape(talk_experts * talk_capacity, talk_features)
    talker_branch = combine_rows(talk_returned, talk_target, talk_weight)
    return (thinker_branch, talker_branch)


def dense_weights(route, weights, experts):
    picks, rows = route.shape
    spot = lax.broadcasted_iota(jnp.int32, (LANES, rows), 0)
    norm = weights / jnp.sum(weights, axis=0, keepdims=True)
    parts = jnp.zeros((LANES, rows), F32)
    for k in range(picks):
        value = norm[k : k + 1]
        high = value.astype(BF16).astype(F32)
        middle = (value - high).astype(BF16).astype(F32)
        low = value - high - middle
        chosen = route[k : k + 1]
        parts = parts + jnp.where(spot == chosen, high, 0.0)
        parts = parts + jnp.where(spot == chosen + experts, middle, 0.0)
        parts = parts + jnp.where(spot == chosen + 2 * experts, low, 0.0)
    down = lax.broadcasted_iota(jnp.int32, (rows, rows), 0)
    along = lax.broadcasted_iota(jnp.int32, (rows, rows), 1)
    turned = lax.dot_general(
        jnp.where(down == along, 1.0, 0.0).astype(BF16), parts.astype(BF16),
        (((1,), (1,)), ((), ())), preferred_element_type=F32,
    )
    return turned.astype(BF16)


class Place:
    def __init__(self, layers):
        self.layers = layers
        self.ep = lax.axis_index("ep")
        self.z = self.ep // 4
        self.x = (self.ep // 2) % 2
        self.c = self.ep % 2
        self.sibling = {"ep": self.ep + 1 - 2 * self.c}
        self.across = {"ep": self.ep + 2 - 4 * self.x}
        self.up = {"ep": self.ep + 4}
        self.down = {"ep": self.ep - 4}
        self.has_up = self.z < layers - 1
        self.has_down = self.z > 0


def remote(src, dst, send_sem, recv_sem, peer):
    return pltpu.make_async_remote_copy(
        src_ref=src,
        dst_ref=dst,
        send_sem=send_sem,
        recv_sem=recv_sem,
        device_id=peer,
        device_id_type=pl.DeviceIdType.MESH,
    )


def greet(place):
    barrier = pltpu.get_barrier_semaphore()

    def signal(peer):
        pl.semaphore_signal(barrier, inc=1, device_id=peer, device_id_type=pl.DeviceIdType.MESH)

    signal(place.sibling)
    signal(place.across)

    @pl.when(place.has_up)
    def _():
        signal(place.up)

    @pl.when(place.has_down)
    def _():
        signal(place.down)

    count = 2 + jnp.where(place.has_up, 1, 0) + jnp.where(place.has_down, 1, 0)
    pl.semaphore_wait(barrier, count)


def mixture_phase(place, features, gate_w, up_w, down_w, wait_weights, scratch):
    (held, hidden, scaled, partial, core_in, x_out, x_in, z_out, z_in,
     zs, zr, xs, xr, cs, cr, rs_cs, rs_cr, rs_xs, rs_xr, rs_zs, rs_zr) = scratch
    z, x, c, layers = place.z, place.x, place.c, place.layers
    rows = held.shape[3]
    group = 2 * layers * rows
    ff = gate_w.shape[1]

    def z_copy(way, step, block):
        slot = held.at[x, c, block]
        return remote(slot, slot, zs.at[way, step], zr.at[way, step], (place.up, place.down)[way])

    def x_copy(side, block):
        slot = held.at[side, c, block]
        return remote(slot, slot, xs.at[block], xr.at[block], place.across)

    def c_copy(side, core, block):
        slot = held.at[side, core, block]
        return remote(slot, slot, cs.at[side, block], cr.at[side, block], place.sibling)

    def fan(block):
        x_copy(x, block).start()
        c_copy(x, c, block).start()

    def arrivals(step, then):
        @pl.when(z - 1 - step >= 0)
        def _():
            then(0, z - 1 - step)

        @pl.when(z + 1 + step < layers)
        def _():
            then(1, z + 1 + step)

    def from_across(block):
        x_copy(1 - x, block).wait_recv()
        c_copy(1 - x, c, block).start()

    ahead = (place.has_up, place.has_down)
    for way in range(2):
        @pl.when(ahead[way])
        def _(way=way):
            z_copy(way, 0, z).start()

    fan(z)
    for step in range(layers - 1):
        def pass_on(way, block, step=step):
            z_copy(way, step, block).wait_recv()

            @pl.when(ahead[way])
            def _():
                z_copy(way, step + 1, block).start()

            fan(block)

        arrivals(step, pass_on)
        if step == 0:
            from_across(z)
        else:
            arrivals(step - 1, lambda way, block: from_across(block))

    def from_sibling(side):
        for block in range(layers):
            c_copy(side, 1 - c, block).wait_recv()

    def enter(side, which):
        def tile(i, carry):
            at = pl.ds(pl.multiple_of(i * width, width), width)
            slab = held[side, :, :, :, :features].reshape(group, features)
            gate = jnp.dot(slab, gate_w[:, at], preferred_element_type=F32)
            upper = jnp.dot(slab, up_w[:, at], preferred_element_type=F32)
            hidden[which, :, at] = (gate * (1.0 / (1.0 + jnp.exp(-gate))) * upper).astype(BF16)
            return carry

        width = TILE if ff % TILE == 0 else LANES
        lax.fori_loop(0, ff // width, tile, 0)
        parts = held[side, :, :, :, features:].reshape(group, LANES).astype(F32)
        lane = lax.broadcasted_iota(jnp.int32, (group, LANES), 1)
        experts = 4 * layers
        mine = (lane % experts == place.ep) & (lane < 3 * experts)
        scaled[which] = jnp.sum(jnp.where(mine, parts, 0.0), axis=1, keepdims=True)

    def leave(side, which):
        def tile(i, carry):
            at = pl.ds(pl.multiple_of(i * TILE, TILE), TILE)
            out = jnp.dot(hidden[which], down_w[:, at], preferred_element_type=F32)
            out = (out * scaled[which]).astype(BF16)
            partial[side, :, :, :, at] = out.reshape(2, layers, rows, TILE)
            return carry

        lax.fori_loop(0, features // TILE, tile, 0)

    from_sibling(x)
    wait_weights(0)
    enter(x, 0)
    arrivals(layers - 2, lambda way, block: from_across(block))
    from_sibling(1 - x)
    enter(1 - x, 1)
    wait_weights(1)
    leave(1 - x, 1)

    def core_sum(side, which):
        return remote(
            partial.at[side, 1 - c], core_in.at[which], rs_cs.at[which], rs_cr.at[which],
            place.sibling,
        )

    def x_sum(block):
        return remote(
            x_out.at[block], x_in.at[block], rs_xs.at[block], rs_xr.at[block], place.across
        )

    def z_sum(way, block):
        return remote(
            z_out.at[block], z_in.at[way, block], rs_zs.at[block], rs_zr.at[way, block],
            (place.up, place.down)[way],
        )

    def outward(then):
        for far in range(layers - 1, 0, -1):
            @pl.when(z + far < layers)
            def _(far=far):
                then(0, z + far)

            @pl.when(z - far >= 0)
            def _(far=far):
                then(1, z - far)

    core_sum(1 - x, 1).start()
    leave(x, 0)
    core_sum(x, 0).start()
    core_sum(1 - x, 1).wait_recv()

    def send_across(way, block):
        total = partial[1 - x, c, block].astype(F32) + core_in[1, block].astype(F32)
        x_out[block] = total.astype(BF16)
        x_sum(block).start()

    outward(send_across)
    send_across(0, z)
    core_sum(x, 0).wait_recv()

    def chip_total(block):
        total = partial[x, c, block].astype(F32) + core_in[0, block].astype(F32)
        x_sum(block).wait_recv()
        return total + x_in[block].astype(F32)

    behind = (place.has_down, place.has_up)

    def send_along(way, block):
        total = chip_total(block)

        @pl.when(behind[way])
        def _():
            z_sum(way, block).wait_recv()

        z_out[block] = (total + z_in[way, block].astype(F32)).astype(BF16)
        z_sum(way, block).start()

    outward(send_along)
    total = chip_total(z)
    for way in range(2):
        @pl.when(behind[way])
        def _(way=way):
            z_sum(way, z).wait_recv()

        total = total + z_in[way, z].astype(F32)

    def finish():
        for way in range(2):
            @pl.when(ahead[way])
            def _(way=way):
                z_copy(way, 0, z).wait_send()

        for step in range(layers - 1):
            def sent(way, block, step=step):
                @pl.when(ahead[way])
                def _():
                    z_copy(way, step + 1, block).wait_send()

            arrivals(step, sent)
        for block in range(layers):
            x_copy(x, block).wait_send()
            c_copy(x, c, block).wait_send()
            c_copy(1 - x, c, block).wait_send()
            x_sum(block).wait_send()
        core_sum(x, 0).wait_send()
        core_sum(1 - x, 1).wait_send()
        outward(lambda way, block: z_sum(way, block).wait_send())

    return total, finish


def clear_ends(place, z_in):
    for way, has in enumerate((place.has_down, place.has_up)):
        @pl.when(jnp.logical_not(has))
        def _(way=way):
            z_in[way] = jnp.zeros(z_in.shape[1:], z_in.dtype)


PHASE_REFS = 21


def step_kernel(
    layers,
    rows_ref, route_ref, weight_ref, gain_ref, owner_ref, talk_route_ref, talk_weight_ref,
    gate_hbm, up_hbm, down_hbm, proj_hbm, tgate_hbm, tup_hbm, tdown_hbm,
    think_out, talk_out,
    gate_v, up_v, down_v, proj_v, tgate_v, tup_v, tdown_v, load_sem,
    *phases,
):
    place = Place(layers)
    think, talk = phases[:PHASE_REFS], phases[PHASE_REFS:]
    pairs = (
        (gate_hbm.at[0], gate_v), (up_hbm.at[0], up_v), (down_hbm.at[0], down_v),
        (proj_hbm, proj_v),
        (tgate_hbm.at[0], tgate_v), (tup_hbm.at[0], tup_v), (tdown_hbm.at[0], tdown_v),
    )
    loads = [
        pltpu.make_async_copy(src, dst, load_sem.at[i]) for i, (src, dst) in enumerate(pairs)
    ]
    for load in loads:
        load.start()
    experts = 4 * layers
    features = rows_ref.shape[1]
    talk_features = gain_ref.shape[1]
    z, x, c = place.z, place.x, place.c
    held, talk_held = think[0], talk[0]
    held[x, c, z, :, :features] = rows_ref[...]
    held[x, c, z, :, features:] = dense_weights(route_ref[...], weight_ref[...], experts)
    talk_held[x, c, z, :, talk_features:] = dense_weights(
        talk_route_ref[...], talk_weight_ref[...], experts
    )
    clear_ends(place, think[8])
    clear_ends(place, talk[8])
    greet(place)

    def wait_think(stage):
        for load in (loads[:2], loads[2:3])[stage]:
            load.wait()

    def wait_talk(stage):
        for load in (loads[4:6], loads[6:7])[stage]:
            load.wait()

    total, finish_think = mixture_phase(place, features, gate_v, up_v, down_v, wait_think, think)
    branch = total.astype(BF16)
    think_out[...] = branch
    loads[3].wait()
    projected = jnp.dot(branch, proj_v[...], preferred_element_type=F32).astype(BF16)
    count = owner_ref.shape[1]
    spot = lax.broadcasted_iota(jnp.int32, (count, count), 0)
    picker = jnp.where(owner_ref[...] == spot, 1.0, 0.0).astype(BF16)
    own_rows = lax.dot_general(
        picker, projected, (((0,), (0,)), ((), ())), preferred_element_type=F32
    )
    scale = lax.rsqrt(jnp.mean(own_rows * own_rows, axis=1, keepdims=True) + 1e-06)
    talk_held[x, c, z, :, :talk_features] = (own_rows * scale * gain_ref[...]).astype(BF16)
    total, finish_talk = mixture_phase(
        place, talk_features, tgate_v, tup_v, tdown_v, wait_talk, talk
    )
    talk_out[...] = total.astype(BF16)
    finish_think()
    finish_talk()


def hand_over(think_in, talk_in, think_out, talk_out, sem):
    copies = [
        pltpu.make_async_copy(src, dst, sem.at[i])
        for i, (src, dst) in enumerate(((think_in, think_out), (talk_in, talk_out)))
    ]
    for copy in copies:
        copy.start()
    for copy in copies:
        copy.wait()


def phase_scratch(layers, rows, features, ff):
    group = 2 * layers * rows
    dma = pltpu.SemaphoreType.DMA
    block = (layers, rows, features)
    return [
        pltpu.VMEM((2, 2, layers, rows, features + LANES), BF16),
        pltpu.VMEM((2, group, ff), BF16),
        pltpu.VMEM((2, group, 1), F32),
        pltpu.VMEM((2, 2) + block, BF16),
        pltpu.VMEM((2,) + block, BF16),
        pltpu.VMEM(block, BF16),
        pltpu.VMEM(block, BF16),
        pltpu.VMEM(block, BF16),
        pltpu.VMEM((2,) + block, BF16),
        dma((2, layers)), dma((2, layers)),
        dma((layers,)), dma((layers,)),
        dma((2, layers)), dma((2, layers)),
        dma((2,)), dma((2,)),
        dma((layers,)), dma((layers,)),
        dma((layers,)), dma((2, layers)),
    ]


def dense_on_device(
    thinker_rows, think_route, think_weight, think_gate, think_up, think_down, proj_weight,
    owner_map, talk_gain, talk_route, talk_weight, talk_gate, talk_up, talk_down,
):
    layers = lax.axis_size("ep") // 4
    rows, features = thinker_rows.shape
    talk_features, talk_ff = talk_gate.shape[1:]
    ff = think_gate.shape[2]
    vmem = pl.BlockSpec(memory_space=pltpu.VMEM)
    hbm = pl.BlockSpec(memory_space=pl.ANY)
    weights = (think_gate, think_up, think_down, proj_weight, talk_gate, talk_up, talk_down)
    sizes = [w.shape[-2:] for w in weights]
    all_rows = 4 * layers * rows
    outs = (
        jax.ShapeDtypeStruct((rows, features), BF16),
        jax.ShapeDtypeStruct((rows, talk_features), BF16),
    )
    branches = pl.pallas_call(
        functools.partial(step_kernel, layers),
        out_shape=outs,
        in_specs=[vmem] * 7 + [hbm] * 7,
        out_specs=(vmem, vmem),
        scratch_shapes=[pltpu.VMEM(size, BF16) for size in sizes]
        + [pltpu.SemaphoreType.DMA((len(sizes),))]
        + phase_scratch(layers, rows, features, ff)
        + phase_scratch(layers, rows, talk_features, talk_ff),
        compiler_params=pltpu.CompilerParams(
            collective_id=0, has_side_effects=True, vmem_limit_bytes=56 * 1024 * 1024
        ),
        cost_estimate=pl.CostEstimate(
            flops=6 * all_rows * (features * ff + talk_features * talk_ff),
            bytes_accessed=2 * sum(a * b for a, b in sizes),
            transcendentals=all_rows * (ff + talk_ff),
        ),
    )(
        thinker_rows, think_route.T, think_weight.T, talk_gain[None, :], owner_map[None, :],
        talk_route.T, talk_weight.T, *weights,
    )
    return pl.pallas_call(
        hand_over,
        out_shape=outs,
        in_specs=[hbm, hbm],
        out_specs=(hbm, hbm),
        scratch_shapes=[pltpu.SemaphoreType.DMA((2,))],
    )(*branches)


def on_device(*arguments):
    rows, picks = arguments[1].shape
    talk_rows, talk_picks = arguments[9].shape
    ep_count = lax.axis_size("ep")
    whole = lax.axis_size("sess") == 1 and ep_count % 4 == 0 and 3 * ep_count <= LANES
    if whole and ep_count >= 8 and 2 * picks >= ep_count and arguments[0].shape[1] % TILE == 0:
        return dense_on_device(*arguments)
    return packed_on_device(*arguments)


def solution(mesh):
    return jax.shard_map(
        on_device,
        mesh=mesh,
        in_specs=(
            P(("grp", "ep", "sess"), None),
            P(("grp", "ep", "sess"), None),
            P(("grp", "ep", "sess"), None),
            P("ep", None, "sess"),
            P("ep", None, "sess"),
            P("ep", "sess", None),
            P(None, "sess"),
            P(("grp", "ep")),
            P(),
            P(("grp", "ep", "sess"), None),
            P(("grp", "ep", "sess"), None),
            P(("ep", "sess"), None, None),
            P(("ep", "sess"), None, None),
            P(("ep", "sess"), None, None),
        ),
        out_specs=(P(("grp", "ep", "sess"), None), P(("grp", "ep", "sess"), None)),
        check_vma=False,
    )
```
